32 devices in a mesh: rep: 4 (over x, core), shard: 8 (over z, y).
Axes of the slice: x: 2, y: 2, z: 4, core: 2. Of those that a mesh axis runs over, the one named last changes fastest.
Arguments:
- layer_input: bfloat16 [4096, 8192], P(('rep', 'shard')), may hold values from -6 to 6
- queries: bfloat16 [4096, 512], P(('rep', 'shard')), may hold values from -10 to 10
- d_out: bfloat16 [4096, 512], P(('rep', 'shard')), may hold values from -6 to 6
- segment_ids: int32 [32, 128], P(('rep', 'shard')), may hold values from 0 to 3, never falling along the last dimension, each value on 1 to 64 neighbouring positions
- kv_weight: bfloat16 [8192, 256], P('shard'), may hold values from -0.0625 to 0.0625
Outputs:
- d_input: bfloat16 [4096, 8192], P(('rep', 'shard'))
- d_queries: bfloat16 [4096, 512], P(('rep', 'shard'))
- d_kv_weight: float32 [8192, 256], P('shard')
The draws below stay inside these ranges and needn't reach their ends.
All inputs are finite; a program needn't handle non-finite values.
Results may differ from the reference program's by a relative error of at most 0.03.
Values may be sent and summed in bfloat16 or wider, within the bound.
No kernel may reach another device: no remote copies, remote signals or barrier semaphores. Data moves between devices by JAX's collectives and lax.ppermute only.
A program may use at most 64 MiB of HBM per device.

```python
import math
import jax
import jax.numpy as jnp
import numpy as np
from jax import lax

D = 8192
HEAD = 128
QH = 4
TOK_DEV = 128
GROUPS = 32
TOKENS = 4096


def draw_queries(key, part):
    key = jax.random.fold_in(key, 7)
    base = jax.random.fold_in(key, 0)
    values = jnp.clip(jax.random.normal(base, (TOKENS, QH * HEAD), jnp.float32), -6.0, 6.0)
    return values.astype(jnp.bfloat16)


def with_spikes(result, key, source, target, blocks, factor):
    owner, partner = [(jnp.arange(result.shape[dim]) // (result.shape[dim] // blocks)).reshape([-1 if axis == dim else 1 for axis in range(result.ndim)]) for dim in (source, target)]
    chosen = jax.random.permutation(key, blocks)[partner]
    strong = (owner == chosen) | (owner == (partner + blocks // 2) % blocks)
    return jnp.where(strong, factor * result, result)


def steps_of(stream_key, dims, cuts, smallest, largest):
    def one(axis_at, blocks):
        draws = jax.random.uniform(jax.random.fold_in(jax.random.fold_in(stream_key, 6), axis_at), (blocks,), jnp.float32, smallest / len(cuts), largest / len(cuts))
        return jnp.repeat(jnp.exp(draws), dims[axis_at] // blocks).reshape((-1,) + (1,) * (len(dims) - axis_at - 1))

    gain = one(*cuts[0])
    for cut in cuts[1:]:
        gain = gain * one(*cut)
    return gain


def profile(amount, total, most, slope):
    portions = [(1 << 20) // math.isqrt(grade ** slope) + 1 for grade in range(2, amount + 1)]
    surplus, counts = total - most - (amount - 1), [1] * (amount - 1)
    while surplus > 0:
        free = [i for i in range(amount - 1) if counts[i] < most]
        whole, remaining = sum([portions[i] for i in free]), surplus
        for i in free:
            more = min(most - counts[i], max(1, remaining * portions[i] // whole), surplus)
            counts[i] = counts[i] + more
            surplus = surplus - more
    return np.array([most] + counts)


def uneven_parts(key, amount, total, reach, skew):
    if amount == 2:
        one = jax.random.randint(key, (), max(1, total - reach), min(reach, total - 1) + 1)
        return jnp.stack([one, total - one])
    sizes = jnp.asarray(profile(amount, total, reach, skew), jnp.int32)
    pairs = (amount - 1) // 2
    source_of, receiver = sizes[1:1 + 2 * pairs:2], sizes[2:2 + 2 * pairs:2]
    room = jnp.minimum(source_of - 1, reach - receiver)
    passed = jax.random.randint(jax.random.fold_in(key, 1), (pairs,), 0, 1 << 20) % (room + 1)
    sizes = sizes.at[1:1 + 2 * pairs:2].set(source_of - passed).at[2:2 + 2 * pairs:2].set(receiver + passed)
    return sizes[jax.random.permutation(jax.random.fold_in(key, 2), amount)]


def normal_values(key, extent, spread, reach, pieces=(), kind=jnp.bfloat16):
    drawn = jax.random.normal(key, extent, jnp.float32) * spread
    if len(pieces) > 0:
        drawn = steps_of(key, extent, pieces, -0.22, 0.18) * drawn
    return jnp.clip(drawn, min=-reach, max=reach).astype(kind)


def noise_with(key, shape, deviation, limit, cuts, heavy, held_as=jnp.bfloat16):
    entries = deviation * jax.random.normal(key, shape, jnp.float32)
    if cuts:
        entries = entries * steps_of(key, shape, cuts, -0.22, 0.18)
    return jnp.clip(with_spikes(entries, jax.random.fold_in(key, 3), *heavy), -limit, limit).astype(held_as)


def setup_inputs(seed: int = 0) -> dict:
    seeds = jax.random.split(jax.random.key(seed), 6)
    return {
        "layer_input": noise_with(seeds[0], (TOKENS, D), 1.0, 6.0, ((0, 32),), (0, 1, 32, 2.75)),
        "queries": draw_queries(jax.random.fold_in(seeds[5], 71), 0),
        "d_out": normal_values(seeds[2], (TOKENS, QH * HEAD), 1.0, 6.0, ((0, 32),)),
        "segment_ids": jax.vmap(lambda own: jnp.searchsorted(jnp.cumsum(uneven_parts(own, 4, TOK_DEV, TOK_DEV // 2, 1)), jnp.arange(TOK_DEV), side="right"))(jax.random.split(seeds[3], GROUPS)).reshape((GROUPS, TOK_DEV)).astype(jnp.int32),
        "kv_weight": normal_values(seeds[4], (D, 2 * HEAD), D ** -0.5, 0.0625, ((0, 8),)),
    }


def attention_grad(queries, keyval, d_out, segment):
    rows = queries.shape[0]
    scale = 1.0 / HEAD ** 0.5
    heads = queries.reshape(rows, QH, HEAD).astype(jnp.float32)
    grads = d_out.reshape(rows, QH, HEAD).astype(jnp.float32)
    keys = keyval[:, :HEAD].astype(jnp.float32)
    values = keyval[:, HEAD:].astype(jnp.float32)
    position = jnp.arange(rows)
    allowed = (segment[:, None] == segment[None, :]) & (position[None, :] <= position[:, None])
    scores = jnp.einsum('thd,sd->hts', heads, keys) * scale
    scores = jnp.where(allowed[None], scores, -1e+30)
    top = lax.optimization_barrier(jnp.max(scores, axis=2, keepdims=True))
    weights = jnp.where(allowed[None], jnp.exp(scores - top), 0.0)
    probs = weights / lax.optimization_barrier(jnp.sum(weights, axis=2, keepdims=True))
    probs_low = probs.astype(jnp.bfloat16).astype(jnp.float32)
    attended = jnp.einsum('hts,sd->thd', probs_low, values)
    delta = lax.optimization_barrier(jnp.sum(grads * attended, axis=2))
    dprob = jnp.einsum('thd,sd->hts', grads, values)
    dscore = (probs * (dprob - jnp.transpose(delta)[:, :, None])).astype(jnp.bfloat16).astype(jnp.float32)
    d_queries = (jnp.einsum('hts,sd->thd', dscore, keys) * scale).astype(jnp.bfloat16)
    d_keys = jnp.einsum('hts,thd->sd', dscore, heads) * scale
    d_values = jnp.einsum('hts,thd->sd', probs_low, grads)
    d_keyval = jnp.concatenate([d_keys, d_values], axis=1).astype(jnp.bfloat16)
    return (d_queries.reshape(rows, QH * HEAD), d_keyval)

def reference(layer_input, queries, d_out, segment_ids, kv_weight):
    keyval = jnp.dot(layer_input, kv_weight, preferred_element_type=jnp.float32).astype(jnp.bfloat16)
    blocks = (queries.reshape(GROUPS, TOK_DEV, QH * HEAD), keyval.reshape(GROUPS, TOK_DEV, 2 * HEAD), d_out.reshape(GROUPS, TOK_DEV, QH * HEAD), segment_ids)
    d_queries, d_keyval = lax.map(lambda b: attention_grad(b[0], b[1], b[2], b[3]), blocks)
    d_queries = d_queries.reshape(TOKENS, QH * HEAD)
    d_keyval = d_keyval.reshape(TOKENS, 2 * HEAD)
    d_input = lax.dot_general(d_keyval, kv_weight, (((1,), (1,)), ((), ())), preferred_element_type=jnp.float32).astype(jnp.bfloat16)
    inputs3 = layer_input.reshape(GROUPS, TOK_DEV, D)
    grads3 = d_keyval.reshape(GROUPS, TOK_DEV, 2 * HEAD)

    def accumulate(total, pair):
        term = lax.dot_general(pair[0], pair[1], (((0,), (0,)), ((), ())), preferred_element_type=jnp.float32)
        low = lax.optimization_barrier(term.astype(jnp.bfloat16))
        return (total + low.astype(jnp.float32), None)
    d_kv_weight, _ = lax.scan(accumulate, jnp.zeros((D, 2 * HEAD), jnp.float32), (inputs3, grads3))
    return (d_input, d_queries, d_kv_weight)
```

```python
import functools

import jax
import jax.numpy as jnp
from jax import lax
from jax.experimental import pallas as pl
from jax.experimental.pallas import tpu as pltpu
from jax.sharding import PartitionSpec as P

HEAD = 128
QH = 4
SCALE = 1.0 / HEAD**0.5
NEAR = 2
FRONT = 30 * 10**9
SLIGHT = 5 * 10**9
F32 = jnp.float32
BF16 = jnp.bfloat16
VMEM = pl.BlockSpec(memory_space=pltpu.VMEM)
HBM = pl.BlockSpec(memory_space=pltpu.HBM)
ANY = pl.BlockSpec(memory_space=pl.ANY)
PARAMS = pltpu.CompilerParams(vmem_limit_bytes=24 * 1024 * 1024)


def dot(a, b, dims):
    return lax.dot_general(a, b, (dims, ((), ())), preferred_element_type=F32)


class Plan:
    def __init__(self, ranks, shards, rows, width, deep, cols):
        self.ranks, self.shards = ranks, shards
        self.rows, self.width, self.deep, self.cols = rows, width, deep, cols
        self.group = min(4, ranks, deep // 128)
        self.half = deep // 2
        self.part = deep // self.group
        self.far = shards - NEAR
        self.blocks = min(1, self.group - 2)
        self.near_width = NEAR * self.half
        self.far_width = self.far * self.part

    def sub(self, rank):
        return (rank // 2) % (self.group // 2)

    def half_at(self, shard, rank):
        return shard * self.deep + (rank % 2) * self.half

    def part_at(self, shard, rank):
        return self.half_at(shard, rank) + self.sub(rank) * self.part


def lanes(ref, start, size):
    if not isinstance(start, int):
        start = pl.multiple_of(start, 128)
    return ref.at[:, pl.ds(start, size)]


def launch(pairs, sems):
    copies = [pltpu.make_async_copy(a, b, sems.at[i]) for i, (a, b) in enumerate(pairs)]
    for copy in copies:
        copy.start()
    return copies


def finish(copies):
    for copy in copies:
        copy.wait()


def cut_kernel(plan, x, weight, half, part, *refs):
    outs, sems = refs[:-1], refs[-1]
    r, s = lax.axis_index("rep"), lax.axis_index("shard")
    begin = pl.multiple_of(plan.half_at(0, r), plan.half)
    inner = pl.multiple_of(plan.part_at(0, r), plan.part)
    pairs = [(weight.at[pl.ds(inner, plan.part)], part), (weight.at[pl.ds(begin, plan.half)], half)]
    for d in range(2, plan.group):
        block = outs[0].at[(d - 2) * plan.rows : (d - 1) * plan.rows]
        for e in range(plan.far):
            source = lanes(x, plan.part_at(s ^ (e + NEAR), r ^ d), plan.part)
            pairs.append((source, lanes(block, e * plan.part, plan.part)))
    finish(launch(pairs, sems))


def columns(plan, x, out, r, s):
    pairs = []
    for e in range(NEAR):
        source = lanes(x, plan.half_at(s ^ e, r), plan.half)
        pairs.append((source, lanes(out, e * plan.half, plan.half)))
    for e in range(plan.far):
        source = lanes(x, plan.part_at(s ^ (e + NEAR), r), plan.part)
        pairs.append((source, lanes(out, plan.near_width + e * plan.part, plan.part)))
    return pairs


def stage_kernel(plan, x, q, do, seg_col, seg_row, own, qs, dos, mask, partner, *refs):
    outs, sems = refs[:-1], refs[-1]
    rows = plan.rows
    r, s = lax.axis_index("rep"), lax.axis_index("shard")
    pairs = columns(plan, x, partner, r ^ 1, s)
    for d in range(2, plan.group):
        for e in range(NEAR):
            source = lanes(x, plan.part_at(s ^ e, r ^ d), plan.part)
            pairs.append((source, lanes(outs[d - 2], e * plan.part, plan.part)))
    pairs += columns(plan, x, own, r, s)
    for h in range(QH):
        pairs.append((lanes(q, h * HEAD, HEAD), qs.at[h * rows : (h + 1) * rows]))
        pairs.append((lanes(do, h * HEAD, HEAD), dos.at[h * rows : (h + 1) * rows]))
    copies = launch(pairs, sems)
    to = lax.broadcasted_iota(jnp.int32, (rows, rows), 0)
    of = lax.broadcasted_iota(jnp.int32, (rows, rows), 1)
    allowed = (seg_col[...] == seg_row[...]) & (of <= to)
    mask[...] = allowed.astype(F32)
    finish(copies)


def project_kernel(plan, own, partner, *refs):
    rows, half, part = plan.rows, plan.half, plan.part
    crossed, refs = refs[: plan.blocks], refs[plan.blocks :]
    near, refs = refs[:NEAR], refs[NEAR:]
    far, outs = refs[: plan.far], refs[plan.far :]
    both = jnp.zeros((2 * rows, plan.cols), F32)
    for e in range(NEAR):
        span = slice(e * half, (e + 1) * half)
        left = jnp.concatenate([own[:, span], partner[:, span]], axis=0)
        both += dot(left, near[e][...], ((1,), (0,)))
    wide = jnp.zeros(((2 + plan.blocks) * rows, plan.cols), F32)
    for e in range(plan.far):
        span = slice(e * part, (e + 1) * part)
        shifted = slice(plan.near_width + e * part, plan.near_width + (e + 1) * part)
        left = [own[:, shifted], partner[:, shifted]] + [o[:rows, span] for o in crossed]
        wide += dot(jnp.concatenate(left, axis=0), far[e][...], ((1,), (0,)))
    outs[0][...] = both[:rows] + wide[:rows]
    outs[1][...] = (both[rows:] + wide[rows : 2 * rows]).astype(BF16)
    for out in outs[2:]:
        out[...] = wide[2 * rows :].astype(BF16)


def project_last_kernel(plan, after, handed, *refs):
    far, out = refs[: plan.far], refs[-1]
    wide = jnp.zeros(out.shape, F32)
    for e in range(plan.far):
        left = handed[:, e * plan.part : (e + 1) * plan.part]
        wide += dot(left, far[e][...], ((1,), (0,)))
    out[...] = wide.astype(BF16)


def attention_kernel(group, qs_ref, dos_ref, mask, *refs):
    terms, (dq, dkv) = refs[:group], refs[-2:]
    rows = mask.shape[0]
    keyval = terms[0][...]
    for term in terms[1:]:
        keyval += term[...].astype(F32)
    keys = keyval[:, :HEAD].astype(BF16)
    values = keyval[:, HEAD:].astype(BF16)
    allowed = jnp.concatenate([mask[...]] * QH, axis=0) > 0.5
    qs, dos = qs_ref[...], dos_ref[...]
    scores = dot(qs, keys, ((1,), (1,))) * SCALE
    dprob = dot(dos, values, ((1,), (1,)))
    scores = jnp.where(allowed, scores, -1e30)
    top = jnp.max(scores, axis=1, keepdims=True)
    weights = jnp.where(allowed, jnp.exp(scores - top), 0.0)
    probs = weights / jnp.sum(weights, axis=1, keepdims=True)
    low = probs.astype(BF16)
    delta = jnp.sum(low.astype(F32) * dprob, axis=1, keepdims=True)
    dscore = (probs * (dprob - delta)).astype(BF16)
    d_keys = dot(dscore, qs, ((0,), (0,)))
    d_values = dot(low, dos, ((0,), (0,)))
    dkv[:, :HEAD] = (d_keys * SCALE).astype(BF16)
    dkv[:, HEAD:] = d_values.astype(BF16)
    d_queries = (dot(dscore, keys, ((1,), (0,))) * SCALE).astype(BF16)
    for h in range(QH):
        dq[:, h * HEAD : (h + 1) * HEAD] = d_queries[h * rows : (h + 1) * rows]


def weight_grad_kernel(plan, shards, own, partner, *refs):
    group, rows, part, half = plan.group, plan.rows, plan.part, plan.half
    others, refs = refs[: group - 2], refs[group - 2 :]
    grads, outs = refs[:group], refs[group:]
    r = lax.axis_index("rep")
    grad = jnp.concatenate([g[...] for g in grads], axis=0)
    inner = plan.sub(r) * part
    for e, (index, row) in shards.items():
        if e < NEAR:
            at = pl.multiple_of(e * half + inner, 128)
            span = slice(e * part, (e + 1) * part)
            left = [own[:, pl.ds(at, part)], partner[:, pl.ds(at, part)]]
        else:
            start = (e - NEAR) * part
            span = slice(start, start + part)
            shifted = slice(plan.near_width + start, plan.near_width + start + part)
            left = [own[:, shifted], partner[:, shifted]]
        left += [o[:rows, span] for o in others]
        term = dot(jnp.concatenate(left, axis=0), grad, ((0,), (0,))).astype(BF16)
        outs[index][row * part : (row + 1) * part] = term


def gather_kernel(plan, after, *refs):
    far, out = refs[: plan.far], refs[plan.far]
    for e in range(plan.far):
        out[e * plan.part : (e + 1) * plan.part] = far[e][...]


def input_grad_kernel(plan, after, grad, other, *refs):
    rows, half, part = plan.rows, plan.half, plan.part
    near, refs = refs[:NEAR], refs[NEAR:]
    far, outs = refs[: 1 + plan.blocks], refs[1 + plan.blocks :]
    r = lax.axis_index("rep")
    both = jnp.concatenate([grad[...], other[...]], axis=0)
    for e in range(NEAR):
        span = slice(e * half, (e + 1) * half)
        term = dot(both, near[e][...], ((1,), (1,))).astype(BF16)
        outs[0][:, span] = term[:rows]
        outs[1][:, span] = term[rows:]
    for e in range(plan.far):
        for i, piece in enumerate(far):
            sub = plan.sub(r) if i == 0 else 1 - plan.sub(r)
            at = pl.multiple_of((NEAR + e) * half + sub * part, 128)
            term = dot(both, piece[e * part : (e + 1) * part], ((1,), (1,))).astype(BF16)
            outs[0][:, pl.ds(at, part)] = term[:rows]
            outs[1][:, pl.ds(at, part)] = term[rows:]


def place_kernel(plan, mine, came, out, sems):
    r, s = lax.axis_index("rep"), lax.axis_index("shard")
    pairs = []
    for d, ref in enumerate((mine, came)):
        for e in range(plan.shards):
            target = lanes(out, plan.half_at(s ^ e, r ^ d), plan.half)
            pairs.append((lanes(ref, e * plan.half, plan.half), target))
    finish(launch(pairs, sems))


def pair_kernel(mine, came, out):
    out[...] = (mine[...].astype(F32) + came[...].astype(F32)).astype(BF16)


def near_kernel(mine, other, came, keep, send):
    rows = mine.shape[0]
    keep[...] = mine[...].astype(F32) + came[:rows].astype(F32)
    send[...] = (other[...].astype(F32) + came[rows:].astype(F32)).astype(BF16)


def total_kernel(mine, *refs):
    total = mine[...].astype(F32)
    for ref in refs[:-1]:
        total += ref[...].astype(F32)
    refs[-1][...] = total.astype(refs[-1].dtype)


def rows_kernel(plan, flips, *refs):
    terms, (out, wide, sems) = refs[-3 - len(flips) : -3], refs[-3:]
    r = lax.axis_index("rep")
    pairs = []
    for i, (flip, term) in enumerate(zip(flips, terms)):
        wide[i * plan.part : (i + 1) * plan.part] = term[...].astype(F32)
        start = pl.multiple_of(plan.part_at(0, r ^ flip), plan.part)
        pairs.append((wide.at[i * plan.part : (i + 1) * plan.part], out.at[pl.ds(start, plan.part)]))
    finish(launch(pairs, sems))


def hand_on_kernel(after, block, out):
    rows = out.shape[0]
    out[...] = block[rows:]


def nothing(*refs):
    pass


def gate(array, *waits, weight=0, spec=ANY):
    operand = pltpu.with_memory_space_constraint(array, pltpu.VMEM)
    if spec is HBM:
        waits = [pltpu.with_memory_space_constraint(wait, pltpu.HBM) for wait in waits]
    return pl.pallas_call(
        nothing,
        out_shape=pltpu.VMEM(array.shape, array.dtype),
        in_specs=[VMEM] + [spec] * len(waits),
        out_specs=VMEM,
        input_output_aliases={0: 0},
        compiler_params=PARAMS,
        cost_estimate=pl.CostEstimate(flops=weight, bytes_accessed=0, transcendentals=0),
        name="gate",
    )(operand, *waits)


def call(kernel, name, ins, in_specs, shapes, out_spec, scratch=(), copies=0, loose=0, weight=0, alias=()):
    sems = [pltpu.SemaphoreType.DMA((copies,))] if copies else []
    spaces = {id(HBM): pltpu.HBM, id(VMEM): pltpu.VMEM}
    ins = [
        pltpu.with_memory_space_constraint(a, spaces[id(spec)]) if id(spec) in spaces else a
        for a, spec in zip(ins, in_specs)
    ]
    shapes = [pltpu.VMEM(a.shape, a.dtype) if i >= loose else a for i, a in enumerate(shapes)]
    return pl.pallas_call(
        kernel,
        out_shape=tuple(shapes),
        in_specs=in_specs,
        out_specs=tuple([out_spec] * len(shapes)),
        scratch_shapes=list(scratch) + sems,
        input_output_aliases=dict(alias),
        compiler_params=PARAMS,
        cost_estimate=pl.CostEstimate(flops=weight, bytes_accessed=0, transcendentals=0),
        name=name,
    )(*ins)


def body(ranks, shards, layer_input, queries, d_out, segment_ids, kv_weight):
    rows, width = layer_input.shape
    deep, cols = kv_weight.shape
    plan = Plan(ranks, shards, rows, width, deep, cols)
    group, half, part = plan.group, plan.half, plan.part
    lines = shards // 2
    r = lax.axis_index("rep")
    shape = jax.ShapeDtypeStruct

    def swap(array, axis, flip):
        size = ranks if axis == "rep" else shards
        return lax.ppermute(array, axis, [(i, i ^ flip) for i in range(size)])

    full = shape((rows, plan.near_width + plan.far_width), BF16)
    others = group - 2
    blocks = plan.blocks
    cuts = call(
        functools.partial(cut_kernel, plan), "cut", [layer_input, kv_weight], [HBM] * 2,
        [shape((half, cols), BF16), shape((part, cols), BF16)]
        + [shape((others * rows, plan.far_width), BF16)] * blocks,
        VMEM, copies=2 + others * plan.far,
    )
    own_half, own_part = cuts[:2]

    def hand_on(block, after, weight):
        half_block = shape((rows, block.shape[1]), BF16)
        mine = call(
            hand_on_kernel, "hand_on", [after, block], [ANY, VMEM], [half_block], VMEM, weight=weight
        )[0]
        return [block, swap(mine, "rep", 1)]

    def write(flips, terms, given=(), waits=()):
        return call(
            functools.partial(rows_kernel, plan, flips), "rows", [*given, *waits, *terms],
            [HBM] * len(given) + [ANY] * len(waits) + [VMEM] * len(terms),
            [shape((deep, cols), F32)], HBM,
            scratch=[pltpu.VMEM((len(flips) * part, cols), F32)], copies=len(flips), loose=1,
            alias={0: 0} if given else {},
        )[0]

    def cross(pieces, *waits):
        return [swap(gate(p, *waits) if waits else p, "rep", 2) for p in pieces]

    far_cross = cross(cuts[2:])
    beside = swap(own_half, "shard", 1)
    ahead = swap(own_part, "shard", 2)
    apart = [swap(own_part, "shard", 2 * d) for d in range(2, lines)]
    near = [own_half, beside]
    far = [a for piece in (ahead, *apart) for a in (piece, swap(piece, "shard", 1))]
    corner = far[1]
    far_x = []
    for block in far_cross:
        far_x += hand_on(block, corner, FRONT)

    stacked = shape((QH * rows, HEAD), BF16)
    staged = call(
        functools.partial(stage_kernel, plan), "stage",
        [layer_input, queries, d_out, segment_ids.reshape(rows, 1), segment_ids],
        [HBM] * 3 + [VMEM] * 2,
        [full, stacked, stacked, shape((rows, rows), F32), full]
        + [shape((rows, NEAR * part), BF16)] * others,
        VMEM, copies=2 * shards + others * NEAR + 2 * QH, weight=SLIGHT,
    )
    own, qs, dos, mask = staged[:4]
    partner = swap(gate(staged[4], apart[0], corner, beside), "rep", 1)

    low = shape((rows, cols), BF16)
    terms = list(call(
        functools.partial(project_kernel, plan), "project",
        [own, partner, *far_x[:1], *near, *far], [VMEM] * (2 + blocks + NEAR + plan.far),
        [shape((rows, cols), F32)] + [low] * (1 + blocks), VMEM, weight=FRONT,
    ))
    for handed in far_x[1:]:
        terms += call(
            functools.partial(project_last_kernel, plan), "project_last",
            [terms[0], handed, *far], [ANY] + [VMEM] * (1 + plan.far), [low], VMEM,
        )
    terms = [terms[0]] + [swap(terms[d], "rep", d) for d in range(1, group)]

    d_queries, d_keyval = call(
        functools.partial(attention_kernel, group), "attention",
        [qs, dos, mask, *terms], [VMEM] * (3 + group),
        [shape(queries.shape, BF16), shape((rows, cols), BF16)], VMEM, loose=1, weight=FRONT,
    )

    grads = [d_keyval] + [swap(d_keyval, "rep", d) for d in range(1, group)]
    block = shape((part, cols), BF16)
    places = {2: (0, 0), 3: (0, 1), **{e: (e - 3, 0) for e in range(4, shards)}}
    outs = [shape((2 * part, cols), BF16)] + [block] * (shards - 4)
    sums = list(call(
        functools.partial(weight_grad_kernel, plan, places), "weight_grad",
        [own, partner, *far_x, *grads], [VMEM] * (2 * group), outs, VMEM,
    ))
    mine = call(
        functools.partial(gather_kernel, plan), "gather", [sums[0], *far], [ANY] + [VMEM] * plan.far,
        [shape((plan.far * part, cols), BF16)], VMEM,
    )
    far_rows_all = [*mine, *cross(list(mine) * blocks)]
    near_x = [swap(gate(a, d_keyval), "rep", d + 2) for d, a in enumerate(staged[5:])]
    held = []

    beyond = swap(gate(sums[0], *near_x[:1]), "shard", 2)

    def pair(d):
        came = swap(sums[places[2 * d + 1][0]], "shard", 1)
        mine = gate(sums[places[2 * d][0]], *held[-1:], weight=FRONT)
        out = call(pair_kernel, "pair", [mine, came], [VMEM] * 2, [block], VMEM)[0]
        held.append(out)
        return out

    pairs = {d: pair(d) for d in range(2, lines)}
    total = [swap(pairs[d], "shard", 2 * d) for d in range(2, lines)]
    near_terms = call(
        functools.partial(weight_grad_kernel, plan, {0: (0, 0), 1: (1, 0)}), "weight_grad_near",
        [own, partner, *near_x, *grads], [VMEM] * (2 * group), [block] * 2, VMEM,
    )
    keep, send = call(
        near_kernel, "near", [*near_terms, beyond], [VMEM] * 3, [shape((part, cols), F32), block], VMEM
    )
    total.append(swap(gate(send, pairs[lines - 1]), "shard", 1))
    again = ranks > group
    quarter = call(
        total_kernel, "total", [keep, *total], [VMEM] * (1 + len(total)),
        [shape((part, cols), F32 if again else BF16)], VMEM,
    )[0]
    if again:
        rings = [[g + group * k for k in range(ranks // group)] for g in range(group)]
        quarter = lax.psum(quarter, "rep", axis_index_groups=rings).astype(BF16)
    halves = shape((rows, shards * half), BF16)
    backs = call(
        functools.partial(input_grad_kernel, plan), "input_grad",
        [quarter, *grads[:2], *near, *far_rows_all], [ANY] + [VMEM] * (3 + NEAR + blocks),
        [halves] * 2, VMEM,
    )
    backs = [backs[0], swap(backs[1], "rep", 1)]
    quarters = [quarter, swap(quarter, "rep", 1)]
    d_kv_weight = write(range(2), quarters, waits=backs[:1])
    for crossing in cross([quarter] * blocks):
        crossing = gate(crossing, d_kv_weight, weight=FRONT, spec=HBM)
        quarters += [crossing, swap(crossing, "rep", 1)]
    d_input = call(
        functools.partial(place_kernel, plan), "place", backs, [VMEM] * 2,
        [shape((rows, width), BF16)], HBM, copies=2 * shards, loose=1, weight=FRONT,
    )[0]
    if group > 2:
        d_kv_weight = write(range(2, group), quarters[2:], [d_kv_weight, d_input])
    return (d_input, d_queries, d_kv_weight)


def solution(mesh):
    ranks, shards = mesh.shape["rep"], mesh.shape["shard"]
    spread = P(("rep", "shard"), None)
    return jax.shard_map(
        functools.partial(body, ranks, shards),
        mesh=mesh,
        in_specs=(spread, spread, spread, spread, P("shard", None)),
        out_specs=(spread, spread, P("shard", None)),
        check_vma=False,
    )
```

```python
import functools

import jax
import jax.numpy as jnp
from jax import lax
from jax.experimental import pallas as pl
from jax.experimental.pallas import tpu as pltpu
from jax.sharding import PartitionSpec as P

HEAD = 128
QH = 4
SCALE = 1.0 / HEAD**0.5
NEAR = 2
FRONT = 30 * 10**9
SLIGHT = 5 * 10**9
F32 = jnp.float32
BF16 = jnp.bfloat16
VMEM = pl.BlockSpec(memory_space=pltpu.VMEM)
HBM = pl.BlockSpec(memory_space=pltpu.HBM)
ANY = pl.BlockSpec(memory_space=pl.ANY)
PARAMS = pltpu.CompilerParams(vmem_limit_bytes=24 * 1024 * 1024)


def dot(a, b, dims):
    return lax.dot_general(a, b, (dims, ((), ())), preferred_element_type=F32)


class Plan:
    def __init__(self, ranks, shards, rows, width, deep, cols):
        self.ranks, self.shards = ranks, shards
        self.rows, self.width, self.deep, self.cols = rows, width, deep, cols
        self.group = min(4, ranks, deep // 128)
        self.half = deep // 2
        self.part = deep // self.group
        self.far = shards - NEAR
        self.blocks = min(1, self.group - 2)
        self.near_width = NEAR * self.half
        self.far_width = self.far * self.part

    def sub(self, rank):
        return (rank // 2) % (self.group // 2)

    def half_at(self, shard, rank):
        return shard * self.deep + (rank % 2) * self.half

    def part_at(self, shard, rank):
        return self.half_at(shard, rank) + self.sub(rank) * self.part


def lanes(ref, start, size):
    if not isinstance(start, int):
        start = pl.multiple_of(start, 128)
    return ref.at[:, pl.ds(start, size)]


def launch(pairs, sems):
    copies = [pltpu.make_async_copy(a, b, sems.at[i]) for i, (a, b) in enumerate(pairs)]
    for copy in copies:
        copy.start()
    return copies


def finish(copies):
    for copy in copies:
        copy.wait()


def cut_kernel(plan, x, weight, half, part, *refs):
    outs, sems = refs[:-1], refs[-1]
    r, s = lax.axis_index("rep"), lax.axis_index("shard")
    begin = pl.multiple_of(plan.half_at(0, r), plan.half)
    inner = pl.multiple_of(plan.part_at(0, r), plan.part)
    pairs = [(weight.at[pl.ds(inner, plan.part)], part), (weight.at[pl.ds(begin, plan.half)], half)]
    for d in range(2, plan.group):
        block = outs[0].at[(d - 2) * plan.rows : (d - 1) * plan.rows]
        for e in range(plan.far):
            source = lanes(x, plan.part_at(s ^ (e + NEAR), r ^ d), plan.part)
            pairs.append((source, lanes(block, e * plan.part, plan.part)))
    finish(launch(pairs, sems))


def columns(plan, x, out, r, s):
    pairs = []
    for e in range(NEAR):
        source = lanes(x, plan.half_at(s ^ e, r), plan.half)
        pairs.append((source, lanes(out, e * plan.half, plan.half)))
    for e in range(plan.far):
        source = lanes(x, plan.part_at(s ^ (e + NEAR), r), plan.part)
        pairs.append((source, lanes(out, plan.near_width + e * plan.part, plan.part)))
    return pairs


def stage_kernel(plan, x, q, do, seg_col, seg_row, own, qs, dos, mask, partner, *refs):
    outs, sems = refs[:-1], refs[-1]
    rows = plan.rows
    r, s = lax.axis_index("rep"), lax.axis_index("shard")
    pairs = columns(plan, x, partner, r ^ 1, s)
    for d in range(2, plan.group):
        for e in range(NEAR):
            source = lanes(x, plan.part_at(s ^ e, r ^ d), plan.part)
            pairs.append((source, lanes(outs[d - 2], e * plan.part, plan.part)))
    pairs += columns(plan, x, own, r, s)
    for h in range(QH):
        pairs.append((lanes(q, h * HEAD, HEAD), qs.at[h * rows : (h + 1) * rows]))
        pairs.append((lanes(do, h * HEAD, HEAD), dos.at[h * rows : (h + 1) * rows]))
    copies = launch(pairs, sems)
    to = lax.broadcasted_iota(jnp.int32, (rows, rows), 0)
    of = lax.broadcasted_iota(jnp.int32, (rows, rows), 1)
    allowed = (seg_col[...] == seg_row[...]) & (of <= to)
    mask[...] = allowed.astype(F32)
    finish(copies)


def project_kernel(plan, own, partner, *refs):
    rows, half, part = plan.rows, plan.half, plan.part
    crossed, refs = refs[: plan.blocks], refs[plan.blocks :]
    near, refs = refs[:NEAR], refs[NEAR:]
    far, outs = refs[: plan.far], refs[plan.far :]
    both = jnp.zeros((2 * rows, plan.cols), F32)
    for e in range(NEAR):
        span = slice(e * half, (e + 1) * half)
        left = jnp.concatenate([own[:, span], partner[:, span]], axis=0)
        both += dot(left, near[e][...], ((1,), (0,)))
    wide = jnp.zeros(((2 + plan.blocks) * rows, plan.cols), F32)
    for e in range(plan.far):
        span = slice(e * part, (e + 1) * part)
        shifted = slice(plan.near_width + e * part, plan.near_width + (e + 1) * part)
        left = [own[:, shifted], partner[:, shifted]] + [o[:rows, span] for o in crossed]
        wide += dot(jnp.concatenate(left, axis=0), far[e][...], ((1,), (0,)))
    outs[0][...] = both[:rows] + wide[:rows]
    outs[1][...] = (both[rows:] + wide[rows : 2 * rows]).astype(BF16)
    for out in outs[2:]:
        out[...] = wide[2 * rows :].astype(BF16)


def project_last_kernel(plan, after, handed, *refs):
    far, out = refs[: plan.far], refs[-1]
    wide = jnp.zeros(out.shape, F32)
    for e in range(plan.far):
        left = handed[:, e * plan.part : (e + 1) * plan.part]
        wide += dot(left, far[e][...], ((1,), (0,)))
    out[...] = wide.astype(BF16)


def attention_kernel(group, qs_ref, dos_ref, mask, *refs):
    terms, (dq, dkv) = refs[:group], refs[-2:]
    rows = mask.shape[0]
    keyval = terms[0][...]
    for term in terms[1:]:
        keyval += term[...].astype(F32)
    keys = keyval[:, :HEAD].astype(BF16)
    values = keyval[:, HEAD:].astype(BF16)
    allowed = jnp.concatenate([mask[...]] * QH, axis=0) > 0.5
    qs, dos = qs_ref[...], dos_ref[...]
    scores = dot(qs, keys, ((1,), (1,))) * SCALE
    dprob = dot(dos, values, ((1,), (1,)))
    scores = jnp.where(allowed, scores, -1e30)
    top = jnp.max(scores, axis=1, keepdims=True)
    weights = jnp.where(allowed, jnp.exp(scores - top), 0.0)
    probs = weights / jnp.sum(weights, axis=1, keepdims=True)
    low = probs.astype(BF16)
    delta = jnp.sum(low.astype(F32) * dprob, axis=1, keepdims=True)
    dscore = (probs * (dprob - delta)).astype(BF16)
    d_keys = dot(dscore, qs, ((0,), (0,)))
    d_values = dot(low, dos, ((0,), (0,)))
    dkv[:, :HEAD] = (d_keys * SCALE).astype(BF16)
    dkv[:, HEAD:] = d_values.astype(BF16)
    d_queries = (dot(dscore, keys, ((1,), (0,))) * SCALE).astype(BF16)
    for h in range(QH):
        dq[:, h * HEAD : (h + 1) * HEAD] = d_queries[h * rows : (h + 1) * rows]


def weight_grad_kernel(plan, shards, own, partner, *refs):
    group, rows, part, half = plan.group, plan.rows, plan.part, plan.half
    others, refs = refs[: group - 2], refs[group - 2 :]
    grads, outs = refs[:group], refs[-1 - max(index for index, _ in shards.values()) :]
    r = lax.axis_index("rep")
    grad = jnp.concatenate([g[...] for g in grads], axis=0)
    inner = plan.sub(r) * part
    for e, (index, row) in shards.items():
        if e < NEAR:
            at = pl.multiple_of(e * half + inner, 128)
            span = slice(e * part, (e + 1) * part)
            left = [own[:, pl.ds(at, part)], partner[:, pl.ds(at, part)]]
        else:
            start = (e - NEAR) * part
            span = slice(start, start + part)
            shifted = slice(plan.near_width + start, plan.near_width + start + part)
            left = [own[:, shifted], partner[:, shifted]]
        left += [o[:rows, span] for o in others]
        term = dot(jnp.concatenate(left, axis=0), grad, ((0,), (0,))).astype(BF16)
        outs[index][row * part : (row + 1) * part] = term


def gather_kernel(plan, after, *refs):
    far, out = refs[: plan.far], refs[plan.far]
    for e in range(plan.far):
        out[e * plan.part : (e + 1) * plan.part] = far[e][...]


def input_grad_kernel(plan, after, grad, other, *refs):
    rows, half, part = plan.rows, plan.half, plan.part
    near, refs = refs[:NEAR], refs[NEAR:]
    far, outs = refs[: 1 + plan.blocks], refs[1 + plan.blocks :]
    r = lax.axis_index("rep")
    both = jnp.concatenate([grad[...], other[...]], axis=0)
    for e in range(NEAR):
        span = slice(e * half, (e + 1) * half)
        term = dot(both, near[e][...], ((1,), (1,))).astype(BF16)
        outs[0][:, span] = term[:rows]
        outs[1][:, span] = term[rows:]
    for e in range(plan.far):
        for i, piece in enumerate(far):
            sub = plan.sub(r) if i == 0 else 1 - plan.sub(r)
            at = pl.multiple_of((NEAR + e) * half + sub * part, 128)
            term = dot(both, piece[e * part : (e + 1) * part], ((1,), (1,))).astype(BF16)
            outs[0][:, pl.ds(at, part)] = term[:rows]
            outs[1][:, pl.ds(at, part)] = term[rows:]


def place_kernel(plan, mine, came, out, sems):
    r, s = lax.axis_index("rep"), lax.axis_index("shard")
    pairs = []
    for d, ref in enumerate((mine, came)):
        for e in range(plan.shards):
            target = lanes(out, plan.half_at(s ^ e, r ^ d), plan.half)
            pairs.append((lanes(ref, e * plan.half, plan.half), target))
    finish(launch(pairs, sems))


def pair_kernel(mine, came, out):
    out[...] = (mine[...].astype(F32) + came[...].astype(F32)).astype(BF16)


def near_kernel(mine, other, came, keep, send):
    rows = mine.shape[0]
    keep[...] = mine[...].astype(F32) + came[:rows].astype(F32)
    send[...] = (other[...].astype(F32) + came[rows:].astype(F32)).astype(BF16)


def total_kernel(mine, *refs):
    total = mine[...].astype(F32)
    for ref in refs[:-1]:
        total += ref[...].astype(F32)
    refs[-1][...] = total.astype(refs[-1].dtype)


def rows_kernel(plan, flips, *refs):
    terms, (out, wide, sems) = refs[-3 - len(flips) : -3], refs[-3:]
    r = lax.axis_index("rep")
    pairs = []
    for i, (flip, term) in enumerate(zip(flips, terms)):
        wide[i * plan.part : (i + 1) * plan.part] = term[...].astype(F32)
        start = pl.multiple_of(plan.part_at(0, r ^ flip), plan.part)
        pairs.append((wide.at[i * plan.part : (i + 1) * plan.part], out.at[pl.ds(start, plan.part)]))
    finish(launch(pairs, sems))


def hand_on_kernel(after, block, out):
    rows = out.shape[0]
    out[...] = block[rows:]


def nothing(*refs):
    pass


def gate(array, *waits, weight=0, spec=ANY):
    operand = pltpu.with_memory_space_constraint(array, pltpu.VMEM)
    if spec is HBM:
        waits = [pltpu.with_memory_space_constraint(wait, pltpu.HBM) for wait in waits]
    return pl.pallas_call(
        nothing,
        out_shape=pltpu.VMEM(array.shape, array.dtype),
        in_specs=[VMEM] + [spec] * len(waits),
        out_specs=VMEM,
        input_output_aliases={0: 0},
        compiler_params=PARAMS,
        cost_estimate=pl.CostEstimate(flops=weight, bytes_accessed=0, transcendentals=0),
        name="gate",
    )(operand, *waits)


def call(kernel, name, ins, in_specs, shapes, out_spec, scratch=(), copies=0, loose=0, weight=0, alias=()):
    sems = [pltpu.SemaphoreType.DMA((copies,))] if copies else []
    spaces = {id(HBM): pltpu.HBM, id(VMEM): pltpu.VMEM}
    ins = [
        pltpu.with_memory_space_constraint(a, spaces[id(spec)]) if id(spec) in spaces else a
        for a, spec in zip(ins, in_specs)
    ]
    shapes = [pltpu.VMEM(a.shape, a.dtype) if i >= loose else a for i, a in enumerate(shapes)]
    return pl.pallas_call(
        kernel,
        out_shape=tuple(shapes),
        in_specs=in_specs,
        out_specs=tuple([out_spec] * len(shapes)),
        scratch_shapes=list(scratch) + sems,
        input_output_aliases=dict(alias),
        compiler_params=PARAMS,
        cost_estimate=pl.CostEstimate(flops=weight, bytes_accessed=0, transcendentals=0),
        name=name,
    )(*ins)


def body(ranks, shards, layer_input, queries, d_out, segment_ids, kv_weight):
    rows, width = layer_input.shape
    deep, cols = kv_weight.shape
    plan = Plan(ranks, shards, rows, width, deep, cols)
    group, half, part = plan.group, plan.half, plan.part
    lines = shards // 2
    r = lax.axis_index("rep")
    shape = jax.ShapeDtypeStruct

    def swap(array, axis, flip):
        size = ranks if axis == "rep" else shards
        return lax.ppermute(array, axis, [(i, i ^ flip) for i in range(size)])

    full = shape((rows, plan.near_width + plan.far_width), BF16)
    others = group - 2
    blocks = plan.blocks
    cuts = call(
        functools.partial(cut_kernel, plan), "cut", [layer_input, kv_weight], [HBM] * 2,
        [shape((half, cols), BF16), shape((part, cols), BF16)]
        + [shape((others * rows, plan.far_width), BF16)] * blocks,
        VMEM, copies=2 + others * plan.far,
    )
    own_half, own_part = cuts[:2]

    def hand_on(block, after, weight):
        half_block = shape((rows, block.shape[1]), BF16)
        mine = call(
            hand_on_kernel, "hand_on", [after, block], [ANY, VMEM], [half_block], VMEM, weight=weight
        )[0]
        return [block, swap(mine, "rep", 1)]

    def write(flips, terms, given=(), waits=()):
        return call(
            functools.partial(rows_kernel, plan, flips), "rows", [*given, *waits, *terms],
            [HBM] * len(given) + [ANY] * len(waits) + [VMEM] * len(terms),
            [shape((deep, cols), F32)], HBM,
            scratch=[pltpu.VMEM((len(flips) * part, cols), F32)], copies=len(flips), loose=1,
            alias={0: 0} if given else {},
        )[0]

    def cross(pieces, *waits):
        return [swap(gate(p, *waits) if waits else p, "rep", 2) for p in pieces]

    far_cross = cross(cuts[2:])
    beside = swap(own_half, "shard", 1)
    ahead = swap(own_part, "shard", 2)
    apart = [swap(own_part, "shard", 2 * d) for d in range(2, lines)]
    near = [own_half, beside]
    far = [a for piece in (ahead, *apart) for a in (piece, swap(piece, "shard", 1))]
    corner = far[1]
    far_x = []
    for block in far_cross:
        far_x += hand_on(block, corner, FRONT)

    stacked = shape((QH * rows, HEAD), BF16)
    staged = call(
        functools.partial(stage_kernel, plan), "stage",
        [layer_input, queries, d_out, segment_ids.reshape(rows, 1), segment_ids],
        [HBM] * 3 + [VMEM] * 2,
        [full, stacked, stacked, shape((rows, rows), F32), full]
        + [shape((rows, NEAR * part), BF16)] * others,
        VMEM, copies=2 * shards + others * NEAR + 2 * QH, weight=SLIGHT,
    )
    own, qs, dos, mask = staged[:4]
    partner = swap(gate(staged[4], apart[0], corner, beside), "rep", 1)

    low = shape((rows, cols), BF16)
    terms = list(call(
        functools.partial(project_kernel, plan), "project",
        [own, partner, *far_x[:1], *near, *far], [VMEM] * (2 + blocks + NEAR + plan.far),
        [shape((rows, cols), F32)] + [low] * (1 + blocks), VMEM, weight=FRONT,
    ))
    for handed in far_x[1:]:
        terms += call(
            functools.partial(project_last_kernel, plan), "project_last",
            [terms[0], handed, *far], [ANY] + [VMEM] * (1 + plan.far), [low], VMEM,
        )
    terms = [terms[0]] + [swap(terms[d], "rep", d) for d in range(1, group)]

    near_x = [swap(gate(a, corner), "rep", 2) for a in staged[5:6]]
    d_queries, d_keyval = call(
        functools.partial(attention_kernel, group), "attention",
        [qs, dos, mask, *terms, *near_x], [VMEM] * (3 + group) + [ANY] * blocks,
        [shape(queries.shape, BF16), shape((rows, cols), BF16)], VMEM, loose=1, weight=FRONT,
    )

    grads = [d_keyval] + [swap(d_keyval, "rep", d) for d in range(1, group)]
    block = shape((part, cols), BF16)
    mine = call(
        functools.partial(gather_kernel, plan), "gather", [grads[1], *far], [ANY] + [VMEM] * plan.far,
        [shape((plan.far * part, cols), BF16)], VMEM,
    )
    far_rows_all = [*mine, *cross(list(mine) * blocks)]
    places = {2: (0, 0), 3: (0, 1), **{e: (e - 3, 0) for e in range(4, shards)}}
    outs = [shape((2 * part, cols), BF16)] + [block] * (shards - 4)
    sums = list(call(
        functools.partial(weight_grad_kernel, plan, places), "weight_grad",
        [own, partner, *far_x, *grads], [VMEM] * (2 * group), outs, VMEM, weight=FRONT,
    ))
    near_x += [swap(gate(a, d_keyval), "rep", 3) for a in staged[6:]]
    held = []

    beyond = swap(gate(sums[0], *near_x[1:]), "shard", 2)

    def pair(d):
        term = sums[places[2 * d + 1][0]]
        came = swap(gate(term, *near_x[1:]) if d > 2 else term, "shard", 1)
        mine = gate(sums[places[2 * d][0]], *held[-1:], weight=SLIGHT // 2)
        out = call(pair_kernel, "pair", [mine, came], [VMEM] * 2, [block], VMEM)[0]
        held.append(out)
        return out

    pairs = {d: pair(d) for d in range(2, lines)}
    total = [swap(pairs[d], "shard", 2 * d) for d in range(2, lines)]
    near_terms = call(
        functools.partial(weight_grad_kernel, plan, {0: (0, 0), 1: (1, 0)}), "weight_grad_near",
        [own, partner, *near_x, *grads, pairs[2]], [VMEM] * (2 * group) + [ANY], [block] * 2, VMEM,
    )
    keep, send = call(
        near_kernel, "near", [*near_terms, beyond], [VMEM] * 3, [shape((part, cols), F32), block], VMEM
    )
    total.append(swap(gate(send, pairs[lines - 1]), "shard", 1))
    again = ranks > group
    quarter = call(
        total_kernel, "total", [keep, *total], [VMEM] * (1 + len(total)),
        [shape((part, cols), F32 if again else BF16)], VMEM,
    )[0]
    if again:
        rings = [[g + group * k for k in range(ranks // group)] for g in range(group)]
        quarter = lax.psum(quarter, "rep", axis_index_groups=rings).astype(BF16)
    halves = shape((rows, shards * half), BF16)
    backs = call(
        functools.partial(input_grad_kernel, plan), "input_grad",
        [quarter, *grads[:2], *near, *far_rows_all], [ANY] + [VMEM] * (3 + NEAR + blocks),
        [halves] * 2, VMEM,
    )
    backs = [backs[0], swap(backs[1], "rep", 1)]
    quarters = [quarter, swap(quarter, "rep", 1)]
    d_kv_weight = write(range(2), quarters, waits=backs[:1])
    for crossing in cross([quarter] * blocks):
        crossing = gate(crossing, d_kv_weight, weight=FRONT, spec=HBM)
        quarters += [crossing, swap(crossing, "rep", 1)]
    d_input = call(
        functools.partial(place_kernel, plan), "place", backs, [VMEM] * 2,
        [shape((rows, width), BF16)], HBM, copies=2 * shards, loose=1, weight=FRONT,
    )[0]
    if group > 2:
        d_kv_weight = write(range(2, group), quarters[2:], [d_kv_weight, d_input])
    return (d_input, d_queries, d_kv_weight)


def solution(mesh):
    ranks, shards = mesh.shape["rep"], mesh.shape["shard"]
    spread = P(("rep", "shard"), None)
    return jax.shard_map(
        functools.partial(body, ranks, shards),
        mesh=mesh,
        in_specs=(spread, spread, spread, spread, P("shard", None)),
        out_specs=(spread, spread, P("shard", None)),
        check_vma=False,
    )
```

```python
import functools

import jax
import jax.numpy as jnp
from jax import lax
from jax.experimental import pallas as pl
from jax.experimental.pallas import tpu as pltpu
from jax.sharding import PartitionSpec as P

HEAD = 128
QH = 4
SCALE = 1.0 / HEAD**0.5
NEAR = 2
FRONT = 30 * 10**9
SLIGHT = 5 * 10**9
F32 = jnp.float32
BF16 = jnp.bfloat16
VMEM = pl.BlockSpec(memory_space=pltpu.VMEM)
HBM = pl.BlockSpec(memory_space=pltpu.HBM)
ANY = pl.BlockSpec(memory_space=pl.ANY)
PARAMS = pltpu.CompilerParams(vmem_limit_bytes=24 * 1024 * 1024)


def dot(a, b, dims):
    return lax.dot_general(a, b, (dims, ((), ())), preferred_element_type=F32)


class Plan:
    def __init__(self, ranks, shards, rows, width, deep, cols):
        self.ranks, self.shards = ranks, shards
        self.rows, self.width, self.deep, self.cols = rows, width, deep, cols
        self.group = min(4, ranks, deep // 128)
        self.half = deep // 2
        self.part = deep // self.group
        self.far = shards - NEAR
        self.blocks = min(1, self.group - 2)
        self.near_width = NEAR * self.half
        self.far_width = self.far * self.part

    def sub(self, rank):
        return (rank // 2) % (self.group // 2)

    def half_at(self, shard, rank):
        return shard * self.deep + (rank % 2) * self.half

    def part_at(self, shard, rank):
        return self.half_at(shard, rank) + self.sub(rank) * self.part


def lanes(ref, start, size):
    if not isinstance(start, int):
        start = pl.multiple_of(start, 128)
    return ref.at[:, pl.ds(start, size)]


def launch(pairs, sems):
    copies = [pltpu.make_async_copy(a, b, sems.at[i]) for i, (a, b) in enumerate(pairs)]
    for copy in copies:
        copy.start()
    return copies


def finish(copies):
    for copy in copies:
        copy.wait()


def cut_kernel(plan, x, weight, half, part, *refs):
    outs, sems = refs[:-1], refs[-1]
    r, s = lax.axis_index("rep"), lax.axis_index("shard")
    begin = pl.multiple_of(plan.half_at(0, r), plan.half)
    inner = pl.multiple_of(plan.part_at(0, r), plan.part)
    pairs = [(weight.at[pl.ds(inner, plan.part)], part), (weight.at[pl.ds(begin, plan.half)], half)]
    for d in range(2, plan.group):
        block = outs[0].at[(d - 2) * plan.rows : (d - 1) * plan.rows]
        for e in range(plan.far):
            source = lanes(x, plan.part_at(s ^ (e + NEAR), r ^ d), plan.part)
            pairs.append((source, lanes(block, e * plan.part, plan.part)))
    finish(launch(pairs, sems))


def columns(plan, x, out, r, s):
    pairs = []
    for e in range(NEAR):
        source = lanes(x, plan.half_at(s ^ e, r), plan.half)
        pairs.append((source, lanes(out, e * plan.half, plan.half)))
    for e in range(plan.far):
        source = lanes(x, plan.part_at(s ^ (e + NEAR), r), plan.part)
        pairs.append((source, lanes(out, plan.near_width + e * plan.part, plan.part)))
    return pairs


def stage_kernel(plan, x, q, do, seg_col, seg_row, own, qs, dos, mask, partner, *refs):
    outs, sems = refs[:-1], refs[-1]
    rows = plan.rows
    r, s = lax.axis_index("rep"), lax.axis_index("shard")
    pairs = columns(plan, x, partner, r ^ 1, s)
    for d in range(2, plan.group):
        for e in range(NEAR):
            source = lanes(x, plan.part_at(s ^ e, r ^ d), plan.part)
            pairs.append((source, lanes(outs[d - 2], e * plan.part, plan.part)))
    pairs += columns(plan, x, own, r, s)
    for h in range(QH):
        pairs.append((lanes(q, h * HEAD, HEAD), qs.at[h * rows : (h + 1) * rows]))
        pairs.append((lanes(do, h * HEAD, HEAD), dos.at[h * rows : (h + 1) * rows]))
    copies = launch(pairs, sems)
    to = lax.broadcasted_iota(jnp.int32, (rows, rows), 0)
    of = lax.broadcasted_iota(jnp.int32, (rows, rows), 1)
    allowed = (seg_col[...] == seg_row[...]) & (of <= to)
    mask[...] = allowed.astype(F32)
    finish(copies)


def project_kernel(plan, own, partner, *refs):
    rows, half, part = plan.rows, plan.half, plan.part
    crossed, refs = refs[: plan.blocks], refs[plan.blocks :]
    near, refs = refs[:NEAR], refs[NEAR:]
    far, outs = refs[: plan.far], refs[plan.far :]
    both = jnp.zeros((2 * rows, plan.cols), F32)
    for e in range(NEAR):
        span = slice(e * half, (e + 1) * half)
        left = jnp.concatenate([own[:, span], partner[:, span]], axis=0)
        both += dot(left, near[e][...], ((1,), (0,)))
    wide = jnp.zeros(((2 + plan.blocks) * rows, plan.cols), F32)
    for e in range(plan.far):
        span = slice(e * part, (e + 1) * part)
        shifted = slice(plan.near_width + e * part, plan.near_width + (e + 1) * part)
        left = [own[:, shifted], partner[:, shifted]] + [o[:rows, span] for o in crossed]
        wide += dot(jnp.concatenate(left, axis=0), far[e][...], ((1,), (0,)))
    outs[0][...] = both[:rows] + wide[:rows]
    outs[1][...] = (both[rows:] + wide[rows : 2 * rows]).astype(BF16)
    for out in outs[2:]:
        out[...] = wide[2 * rows :].astype(BF16)


def project_last_kernel(plan, after, handed, *refs):
    far, out = refs[: plan.far], refs[-1]
    wide = jnp.zeros(out.shape, F32)
    for e in range(plan.far):
        left = handed[:, e * plan.part : (e + 1) * plan.part]
        wide += dot(left, far[e][...], ((1,), (0,)))
    out[...] = wide.astype(BF16)


def attention_kernel(group, qs_ref, dos_ref, mask, *refs):
    terms, (dq, dkv) = refs[:group], refs[-2:]
    rows = mask.shape[0]
    keyval = terms[0][...]
    for term in terms[1:]:
        keyval += term[...].astype(F32)
    keys = keyval[:, :HEAD].astype(BF16)
    values = keyval[:, HEAD:].astype(BF16)
    allowed = jnp.concatenate([mask[...]] * QH, axis=0) > 0.5
    qs, dos = qs_ref[...], dos_ref[...]
    scores = dot(qs, keys, ((1,), (1,))) * SCALE
    dprob = dot(dos, values, ((1,), (1,)))
    scores = jnp.where(allowed, scores, -1e30)
    top = jnp.max(scores, axis=1, keepdims=True)
    weights = jnp.where(allowed, jnp.exp(scores - top), 0.0)
    probs = weights / jnp.sum(weights, axis=1, keepdims=True)
    low = probs.astype(BF16)
    delta = jnp.sum(low.astype(F32) * dprob, axis=1, keepdims=True)
    dscore = (probs * (dprob - delta)).astype(BF16)
    d_keys = dot(dscore, qs, ((0,), (0,)))
    d_values = dot(low, dos, ((0,), (0,)))
    dkv[:, :HEAD] = (d_keys * SCALE).astype(BF16)
    dkv[:, HEAD:] = d_values.astype(BF16)
    d_queries = (dot(dscore, keys, ((1,), (0,))) * SCALE).astype(BF16)
    for h in range(QH):
        dq[:, h * HEAD : (h + 1) * HEAD] = d_queries[h * rows : (h + 1) * rows]


def weight_grad_kernel(plan, shards, own, partner, *refs):
    group, rows, part, half = plan.group, plan.rows, plan.part, plan.half
    others, refs = refs[: group - 2], refs[group - 2 :]
    grads, outs = refs[:group], refs[-1 - max(index for index, _ in shards.values()) :]
    r = lax.axis_index("rep")
    grad = jnp.concatenate([g[...] for g in grads], axis=0)
    inner = plan.sub(r) * part
    for e, (index, row) in shards.items():
        if e < NEAR:
            at = pl.multiple_of(e * half + inner, 128)
            span = slice(e * part, (e + 1) * part)
            left = [own[:, pl.ds(at, part)], partner[:, pl.ds(at, part)]]
        else:
            start = (e - NEAR) * part
            span = slice(start, start + part)
            shifted = slice(plan.near_width + start, plan.near_width + start + part)
            left = [own[:, shifted], partner[:, shifted]]
        left += [o[:rows, span] for o in others]
        term = dot(jnp.concatenate(left, axis=0), grad, ((0,), (0,))).astype(BF16)
        outs[index][row * part : (row + 1) * part] = term


def gather_kernel(plan, after, *refs):
    far, out = refs[: plan.far], refs[plan.far]
    for e in range(plan.far):
        out[e * plan.part : (e + 1) * plan.part] = far[e][...]


def input_grad_kernel(plan, after, grad, other, *refs):
    rows, half, part = plan.rows, plan.half, plan.part
    near, refs = refs[:NEAR], refs[NEAR:]
    far, outs = refs[: 1 + plan.blocks], refs[1 + plan.blocks :]
    r = lax.axis_index("rep")
    both = jnp.concatenate([grad[...], other[...]], axis=0)
    for e in range(NEAR):
        span = slice(e * half, (e + 1) * half)
        term = dot(both, near[e][...], ((1,), (1,))).astype(BF16)
        outs[0][:, span] = term[:rows]
        outs[1][:, span] = term[rows:]
    for e in range(plan.far):
        for i, piece in enumerate(far):
            sub = plan.sub(r) if i == 0 else 1 - plan.sub(r)
            at = pl.multiple_of((NEAR + e) * half + sub * part, 128)
            term = dot(both, piece[e * part : (e + 1) * part], ((1,), (1,))).astype(BF16)
            outs[0][:, pl.ds(at, part)] = term[:rows]
            outs[1][:, pl.ds(at, part)] = term[rows:]


def place_kernel(plan, mine, came, out, sems):
    r, s = lax.axis_index("rep"), lax.axis_index("shard")
    pairs = []
    for d, ref in enumerate((mine, came)):
        for e in range(plan.shards):
            target = lanes(out, plan.half_at(s ^ e, r ^ d), plan.half)
            pairs.append((lanes(ref, e * plan.half, plan.half), target))
    finish(launch(pairs, sems))


def pair_kernel(mine, came, out):
    out[...] = (mine[...].astype(F32) + came[...].astype(F32)).astype(BF16)


def near_kernel(mine, other, came, keep, send):
    rows = mine.shape[0]
    keep[...] = mine[...].astype(F32) + came[:rows].astype(F32)
    send[...] = (other[...].astype(F32) + came[rows:].astype(F32)).astype(BF16)


def total_kernel(mine, *refs):
    total = mine[...].astype(F32)
    for ref in refs[:-1]:
        total += ref[...].astype(F32)
    refs[-1][...] = total.astype(refs[-1].dtype)


def rows_kernel(plan, flips, *refs):
    terms, (out, wide, sems) = refs[-3 - len(flips) : -3], refs[-3:]
    r = lax.axis_index("rep")
    pairs = []
    for i, (flip, term) in enumerate(zip(flips, terms)):
        wide[i * plan.part : (i + 1) * plan.part] = term[...].astype(F32)
        start = pl.multiple_of(plan.part_at(0, r ^ flip), plan.part)
        pairs.append((wide.at[i * plan.part : (i + 1) * plan.part], out.at[pl.ds(start, plan.part)]))
    finish(launch(pairs, sems))


def hand_on_kernel(after, block, out):
    rows = out.shape[0]
    out[...] = block[rows:]


def nothing(*refs):
    pass


def gate(array, *waits, weight=0, spec=ANY):
    operand = pltpu.with_memory_space_constraint(array, pltpu.VMEM)
    if spec is HBM:
        waits = [pltpu.with_memory_space_constraint(wait, pltpu.HBM) for wait in waits]
    return pl.pallas_call(
        nothing,
        out_shape=pltpu.VMEM(array.shape, array.dtype),
        in_specs=[VMEM] + [spec] * len(waits),
        out_specs=VMEM,
        input_output_aliases={0: 0},
        compiler_params=PARAMS,
        cost_estimate=pl.CostEstimate(flops=weight, bytes_accessed=0, transcendentals=0),
        name="gate",
    )(operand, *waits)


def call(kernel, name, ins, in_specs, shapes, out_spec, scratch=(), copies=0, loose=0, weight=0, alias=()):
    sems = [pltpu.SemaphoreType.DMA((copies,))] if copies else []
    spaces = {id(HBM): pltpu.HBM, id(VMEM): pltpu.VMEM}
    ins = [
        pltpu.with_memory_space_constraint(a, spaces[id(spec)]) if id(spec) in spaces else a
        for a, spec in zip(ins, in_specs)
    ]
    shapes = [pltpu.VMEM(a.shape, a.dtype) if i >= loose else a for i, a in enumerate(shapes)]
    return pl.pallas_call(
        kernel,
        out_shape=tuple(shapes),
        in_specs=in_specs,
        out_specs=tuple([out_spec] * len(shapes)),
        scratch_shapes=list(scratch) + sems,
        input_output_aliases=dict(alias),
        compiler_params=PARAMS,
        cost_estimate=pl.CostEstimate(flops=weight, bytes_accessed=0, transcendentals=0),
        name=name,
    )(*ins)


def body(ranks, shards, layer_input, queries, d_out, segment_ids, kv_weight):
    rows, width = layer_input.shape
    deep, cols = kv_weight.shape
    plan = Plan(ranks, shards, rows, width, deep, cols)
    group, half, part = plan.group, plan.half, plan.part
    lines = shards // 2
    r = lax.axis_index("rep")
    shape = jax.ShapeDtypeStruct

    def swap(array, axis, flip):
        size = ranks if axis == "rep" else shards
        return lax.ppermute(array, axis, [(i, i ^ flip) for i in range(size)])

    full = shape((rows, plan.near_width + plan.far_width), BF16)
    others = group - 2
    blocks = plan.blocks
    cuts = call(
        functools.partial(cut_kernel, plan), "cut", [layer_input, kv_weight], [HBM] * 2,
        [shape((half, cols), BF16), shape((part, cols), BF16)]
        + [shape((others * rows, plan.far_width), BF16)] * blocks,
        VMEM, copies=2 + others * plan.far,
    )
    own_half, own_part = cuts[:2]

    def hand_on(block, after, weight):
        half_block = shape((rows, block.shape[1]), BF16)
        mine = call(
            hand_on_kernel, "hand_on", [after, block], [ANY, VMEM], [half_block], VMEM, weight=weight
        )[0]
        return [block, swap(mine, "rep", 1)]

    def write(flips, terms, given=(), waits=()):
        return call(
            functools.partial(rows_kernel, plan, flips), "rows", [*given, *waits, *terms],
            [HBM] * len(given) + [ANY] * len(waits) + [VMEM] * len(terms),
            [shape((deep, cols), F32)], HBM,
            scratch=[pltpu.VMEM((len(flips) * part, cols), F32)], copies=len(flips), loose=1,
            alias={0: 0} if given else {},
        )[0]

    def cross(pieces, *waits):
        return [swap(gate(p, *waits) if waits else p, "rep", 2) for p in pieces]

    far_cross = cross(cuts[2:])
    beside = swap(own_half, "shard", 1)
    ahead = swap(own_part, "shard", 2)
    apart = [swap(own_part, "shard", 2 * d) for d in range(2, lines)]
    near = [own_half, beside]
    far = [a for piece in (ahead, *apart) for a in (piece, swap(piece, "shard", 1))]
    corner = far[1]
    far_x = []
    for block in far_cross:
        far_x += hand_on(block, corner, FRONT)

    stacked = shape((QH * rows, HEAD), BF16)
    staged = call(
        functools.partial(stage_kernel, plan), "stage",
        [layer_input, queries, d_out, segment_ids.reshape(rows, 1), segment_ids],
        [HBM] * 3 + [VMEM] * 2,
        [full, stacked, stacked, shape((rows, rows), F32), full]
        + [shape((rows, NEAR * part), BF16)] * others,
        VMEM, copies=2 * shards + others * NEAR + 2 * QH, weight=SLIGHT,
    )
    own, qs, dos, mask = staged[:4]
    partner = swap(gate(staged[4], apart[0], corner, beside), "rep", 1)

    low = shape((rows, cols), BF16)
    terms = list(call(
        functools.partial(project_kernel, plan), "project",
        [own, partner, *far_x[:1], *near, *far], [VMEM] * (2 + blocks + NEAR + plan.far),
        [shape((rows, cols), F32)] + [low] * (1 + blocks), VMEM, weight=FRONT,
    ))
    for handed in far_x[1:]:
        terms += call(
            functools.partial(project_last_kernel, plan), "project_last",
            [terms[0], handed, *far], [ANY] + [VMEM] * (1 + plan.far), [low], VMEM,
        )
    terms = [terms[0]] + [swap(terms[d], "rep", d) for d in range(1, group)]

    near_x = [swap(gate(a, corner), "rep", 2) for a in staged[5:6]]
    d_queries, d_keyval = call(
        functools.partial(attention_kernel, group), "attention",
        [qs, dos, mask, *terms, *near_x], [VMEM] * (3 + group) + [ANY] * blocks,
        [shape(queries.shape, BF16), shape((rows, cols), BF16)], VMEM, loose=1, weight=FRONT,
    )

    grads = [d_keyval] + [swap(d_keyval, "rep", d) for d in range(1, group)]
    block = shape((part, cols), BF16)
    mine = call(
        functools.partial(gather_kernel, plan), "gather", [grads[1], *far], [ANY] + [VMEM] * plan.far,
        [shape((plan.far * part, cols), BF16)], VMEM,
    )
    far_rows_all = [*mine, *cross(list(mine) * blocks)]
    sums = []
    for places, outs in (
        ({5: (0, 0), 4: (1, 0)}, [block] * 2),
        (
            {2: (0, 0), 3: (0, 1), **{e: (e - 5, 0) for e in range(6, shards)}},
            [shape((2 * part, cols), BF16)] + [block] * (shards - 6),
        ),
    ):
        sums += call(
            functools.partial(weight_grad_kernel, plan, places), "weight_grad",
            [own, partner, *far_x, *grads, *sums], [VMEM] * (2 * group) + [ANY] * len(sums), outs, VMEM,
            weight=0 if sums else FRONT,
        )
    sums = {e: term for e, term in zip((5, 4, 2, *range(6, shards)), sums)}
    near_x += [swap(gate(a, d_keyval), "rep", 3) for a in staged[6:]]
    held = []

    beyond = swap(gate(sums[2], *near_x[1:]), "shard", 2)

    def pair(d):
        term = sums[2 * d + 1]
        came = swap(gate(term, *near_x[1:]) if d > 2 else term, "shard", 1)
        mine = gate(sums[2 * d], *held[-1:], weight=SLIGHT // 2)
        out = call(pair_kernel, "pair", [mine, came], [VMEM] * 2, [block], VMEM)[0]
        held.append(out)
        return out

    pairs = {d: pair(d) for d in range(2, lines)}
    total = [swap(pairs[d], "shard", 2 * d) for d in range(2, lines)]
    near_terms = call(
        functools.partial(weight_grad_kernel, plan, {0: (0, 0), 1: (1, 0)}), "weight_grad_near",
        [own, partner, *near_x, *grads, pairs[2]], [VMEM] * (2 * group) + [ANY], [block] * 2, VMEM,
    )
    keep, send = call(
        near_kernel, "near", [*near_terms, beyond], [VMEM] * 3, [shape((part, cols), F32), block], VMEM
    )
    total.append(swap(gate(send, pairs[lines - 1]), "shard", 1))
    again = ranks > group
    quarter = call(
        total_kernel, "total", [keep, *total], [VMEM] * (1 + len(total)),
        [shape((part, cols), F32 if again else BF16)], VMEM,
    )[0]
    if again:
        rings = [[g + group * k for k in range(ranks // group)] for g in range(group)]
        quarter = lax.psum(quarter, "rep", axis_index_groups=rings).astype(BF16)
    halves = shape((rows, shards * half), BF16)
    backs = call(
        functools.partial(input_grad_kernel, plan), "input_grad",
        [quarter, *grads[:2], *near, *far_rows_all], [ANY] + [VMEM] * (3 + NEAR + blocks),
        [halves] * 2, VMEM,
    )
    backs = [backs[0], swap(backs[1], "rep", 1)]
    quarters = [quarter, swap(quarter, "rep", 1)]
    d_kv_weight = write(range(2), quarters, waits=backs[:1])
    for crossing in cross([quarter] * blocks):
        crossing = gate(crossing, d_kv_weight, weight=FRONT, spec=HBM)
        quarters += [crossing, swap(crossing, "rep", 1)]
    d_input = call(
        functools.partial(place_kernel, plan), "place", backs, [VMEM] * 2,
        [shape((rows, width), BF16)], HBM, copies=2 * shards, loose=1, weight=FRONT,
    )[0]
    if group > 2:
        d_kv_weight = write(range(2, group), quarters[2:], [d_kv_weight, d_input])
    return (d_input, d_queries, d_kv_weight)


def solution(mesh):
    ranks, shards = mesh.shape["rep"], mesh.shape["shard"]
    spread = P(("rep", "shard"), None)
    return jax.shard_map(
        functools.partial(body, ranks, shards),
        mesh=mesh,
        in_specs=(spread, spread, spread, spread, P("shard", None)),
        out_specs=(spread, spread, P("shard", None)),
        check_vma=False,
    )
```

```python
import functools

import jax
import jax.numpy as jnp
from jax import lax
from jax.experimental import pallas as pl
from jax.experimental.pallas import tpu as pltpu
from jax.sharding import PartitionSpec as P

HEAD = 128
QH = 4
SCALE = 1.0 / HEAD**0.5
NEAR = 2
FRONT = 30 * 10**9
SLIGHT = 5 * 10**9
F32 = jnp.float32
BF16 = jnp.bfloat16
VMEM = pl.BlockSpec(memory_space=pltpu.VMEM)
HBM = pl.BlockSpec(memory_space=pltpu.HBM)
ANY = pl.BlockSpec(memory_space=pl.ANY)
PARAMS = pltpu.CompilerParams(vmem_limit_bytes=24 * 1024 * 1024)


def dot(a, b, dims):
    return lax.dot_general(a, b, (dims, ((), ())), preferred_element_type=F32)


class Plan:
    def __init__(self, ranks, shards, rows, width, deep, cols):
        self.ranks, self.shards = ranks, shards
        self.rows, self.width, self.deep, self.cols = rows, width, deep, cols
        self.group = min(4, ranks, deep // 128)
        self.half = deep // 2
        self.part = deep // self.group
        self.far = shards - NEAR
        self.blocks = min(1, self.group - 2)
        self.near_width = NEAR * self.half
        self.far_width = self.far * self.part

    def sub(self, rank):
        return (rank // 2) % (self.group // 2)

    def half_at(self, shard, rank):
        return shard * self.deep + (rank % 2) * self.half

    def part_at(self, shard, rank):
        return self.half_at(shard, rank) + self.sub(rank) * self.part


def lanes(ref, start, size):
    if not isinstance(start, int):
        start = pl.multiple_of(start, 128)
    return ref.at[:, pl.ds(start, size)]


def launch(pairs, sems):
    copies = [pltpu.make_async_copy(a, b, sems.at[i]) for i, (a, b) in enumerate(pairs)]
    for copy in copies:
        copy.start()
    return copies


def finish(copies):
    for copy in copies:
        copy.wait()


def cut_kernel(plan, x, weight, half, part, *refs):
    outs, sems = refs[:-1], refs[-1]
    r, s = lax.axis_index("rep"), lax.axis_index("shard")
    begin = pl.multiple_of(plan.half_at(0, r), plan.half)
    inner = pl.multiple_of(plan.part_at(0, r), plan.part)
    pairs = [(weight.at[pl.ds(inner, plan.part)], part), (weight.at[pl.ds(begin, plan.half)], half)]
    for d in range(2, plan.group):
        block = outs[0].at[(d - 2) * plan.rows : (d - 1) * plan.rows]
        for e in range(plan.far):
            source = lanes(x, plan.part_at(s ^ (e + NEAR), r ^ d), plan.part)
            pairs.append((source, lanes(block, e * plan.part, plan.part)))
    finish(launch(pairs, sems))


def columns(plan, x, out, r, s):
    pairs = []
    for e in range(NEAR):
        source = lanes(x, plan.half_at(s ^ e, r), plan.half)
        pairs.append((source, lanes(out, e * plan.half, plan.half)))
    for e in range(plan.far):
        source = lanes(x, plan.part_at(s ^ (e + NEAR), r), plan.part)
        pairs.append((source, lanes(out, plan.near_width + e * plan.part, plan.part)))
    return pairs


def stage_kernel(plan, x, q, do, seg_col, seg_row, own, qs, dos, mask, partner, *refs):
    outs, sems = refs[:-1], refs[-1]
    rows = plan.rows
    r, s = lax.axis_index("rep"), lax.axis_index("shard")
    pairs = columns(plan, x, partner, r ^ 1, s)
    for d in range(2, plan.group):
        for e in range(NEAR):
            source = lanes(x, plan.part_at(s ^ e, r ^ d), plan.part)
            pairs.append((source, lanes(outs[d - 2], e * plan.part, plan.part)))
    pairs += columns(plan, x, own, r, s)
    for h in range(QH):
        pairs.append((lanes(q, h * HEAD, HEAD), qs.at[h * rows : (h + 1) * rows]))
        pairs.append((lanes(do, h * HEAD, HEAD), dos.at[h * rows : (h + 1) * rows]))
    copies = launch(pairs, sems)
    to = lax.broadcasted_iota(jnp.int32, (rows, rows), 0)
    of = lax.broadcasted_iota(jnp.int32, (rows, rows), 1)
    allowed = (seg_col[...] == seg_row[...]) & (of <= to)
    mask[...] = jnp.where(allowed, 0.0, -1e30)
    finish(copies)


def project_kernel(plan, own, partner, *refs):
    rows, half, part = plan.rows, plan.half, plan.part
    crossed, refs = refs[: plan.blocks], refs[plan.blocks :]
    near, refs = refs[:NEAR], refs[NEAR:]
    far, outs = refs[: plan.far], refs[plan.far :]
    both = jnp.zeros((2 * rows, plan.cols), F32)
    for e in range(NEAR):
        span = slice(e * half, (e + 1) * half)
        left = jnp.concatenate([own[:, span], partner[:, span]], axis=0)
        both += dot(left, near[e][...], ((1,), (0,)))
    wide = jnp.zeros(((2 + plan.blocks) * rows, plan.cols), F32)
    for e in range(plan.far):
        span = slice(e * part, (e + 1) * part)
        shifted = slice(plan.near_width + e * part, plan.near_width + (e + 1) * part)
        left = [own[:, shifted], partner[:, shifted]] + [o[:rows, span] for o in crossed]
        wide += dot(jnp.concatenate(left, axis=0), far[e][...], ((1,), (0,)))
    outs[0][...] = both[:rows] + wide[:rows]
    outs[1][...] = (both[rows:] + wide[rows : 2 * rows]).astype(BF16)
    for out in outs[2:]:
        out[...] = wide[2 * rows :].astype(BF16)


def project_last_kernel(plan, after, handed, *refs):
    far, out = refs[: plan.far], refs[-1]
    wide = jnp.zeros(out.shape, F32)
    for e in range(plan.far):
        left = handed[:, e * plan.part : (e + 1) * plan.part]
        wide += dot(left, far[e][...], ((1,), (0,)))
    out[...] = wide.astype(BF16)


def attention_kernel(group, qs_ref, dos_ref, mask, *refs):
    terms, (dq, dkv) = refs[:group], refs[-2:]
    rows = mask.shape[0]
    keyval = terms[0][...]
    for term in terms[1:]:
        keyval += term[...].astype(F32)
    keys = keyval[:, :HEAD].astype(BF16)
    values = keyval[:, HEAD:].astype(BF16)
    hidden = jnp.concatenate([mask[...]] * QH, axis=0)
    qs, dos = qs_ref[...], dos_ref[...]
    scores = dot(qs, keys, ((1,), (1,))) * SCALE + hidden
    dprob = dot(dos, values, ((1,), (1,)))
    top = jnp.max(scores, axis=1, keepdims=True)
    weights = jnp.exp(scores - top)
    probs = weights / jnp.sum(weights, axis=1, keepdims=True)
    low = probs.astype(BF16)
    delta = jnp.sum(low.astype(F32) * dprob, axis=1, keepdims=True)
    dscore = (probs * (dprob - delta)).astype(BF16)
    d_keys = dot(dscore, qs, ((0,), (0,)))
    d_values = dot(low, dos, ((0,), (0,)))
    dkv[:, :HEAD] = (d_keys * SCALE).astype(BF16)
    dkv[:, HEAD:] = d_values.astype(BF16)
    d_queries = (dot(dscore, keys, ((1,), (0,))) * SCALE).astype(BF16)
    for h in range(QH):
        dq[:, h * HEAD : (h + 1) * HEAD] = d_queries[h * rows : (h + 1) * rows]


def weight_grad_kernel(plan, shards, own, partner, *refs):
    group, rows, part, half = plan.group, plan.rows, plan.part, plan.half
    others, refs = refs[: group - 2], refs[group - 2 :]
    grads, outs = refs[:group], refs[-1 - max(index for index, _ in shards.values()) :]
    r = lax.axis_index("rep")
    grad = jnp.concatenate([g[...] for g in grads], axis=0)
    inner = plan.sub(r) * part
    for e, (index, row) in shards.items():
        if e < NEAR:
            at = pl.multiple_of(e * half + inner, 128)
            span = slice(e * part, (e + 1) * part)
            left = [own[:, pl.ds(at, part)], partner[:, pl.ds(at, part)]]
        else:
            start = (e - NEAR) * part
            span = slice(start, start + part)
            shifted = slice(plan.near_width + start, plan.near_width + start + part)
            left = [own[:, shifted], partner[:, shifted]]
        left += [o[:rows, span] for o in others]
        term = dot(jnp.concatenate(left, axis=0), grad, ((0,), (0,))).astype(BF16)
        outs[index][row * part : (row + 1) * part] = term


def gather_kernel(plan, after, *refs):
    far, out = refs[: plan.far], refs[plan.far]
    for e in range(plan.far):
        out[e * plan.part : (e + 1) * plan.part] = far[e][...]


def input_grad_kernel(plan, after, grad, other, *refs):
    rows, half, part = plan.rows, plan.half, plan.part
    near, refs = refs[:NEAR], refs[NEAR:]
    far, outs = refs[: 1 + plan.blocks], refs[1 + plan.blocks :]
    r = lax.axis_index("rep")
    both = jnp.concatenate([grad[...], other[...]], axis=0)
    for e in range(NEAR):
        span = slice(e * half, (e + 1) * half)
        term = dot(both, near[e][...], ((1,), (1,))).astype(BF16)
        outs[0][:, span] = term[:rows]
        outs[1][:, span] = term[rows:]
    for e in range(plan.far):
        for i, piece in enumerate(far):
            sub = plan.sub(r) if i == 0 else 1 - plan.sub(r)
            at = pl.multiple_of((NEAR + e) * half + sub * part, 128)
            term = dot(both, piece[e * part : (e + 1) * part], ((1,), (1,))).astype(BF16)
            outs[0][:, pl.ds(at, part)] = term[:rows]
            outs[1][:, pl.ds(at, part)] = term[rows:]


def place_kernel(plan, mine, came, out, sems):
    r, s = lax.axis_index("rep"), lax.axis_index("shard")
    pairs = []
    for d, ref in enumerate((mine, came)):
        for e in range(plan.shards):
            target = lanes(out, plan.half_at(s ^ e, r ^ d), plan.half)
            pairs.append((lanes(ref, e * plan.half, plan.half), target))
    finish(launch(pairs, sems))


def pair_kernel(mine, came, out):
    out[...] = (mine[...].astype(F32) + came[...].astype(F32)).astype(BF16)


def near_kernel(mine, other, came, keep, send):
    rows = mine.shape[0]
    keep[...] = mine[...].astype(F32) + came[:rows].astype(F32)
    send[...] = (other[...].astype(F32) + came[rows:].astype(F32)).astype(BF16)


def total_kernel(mine, *refs):
    total = mine[...].astype(F32)
    for ref in refs[:-1]:
        total += ref[...].astype(F32)
    refs[-1][...] = total.astype(refs[-1].dtype)


def rows_kernel(plan, flips, *refs):
    terms, (out, wide, sems) = refs[-3 - len(flips) : -3], refs[-3:]
    r = lax.axis_index("rep")
    pairs = []
    for i, (flip, term) in enumerate(zip(flips, terms)):
        wide[i * plan.part : (i + 1) * plan.part] = term[...].astype(F32)
        start = pl.multiple_of(plan.part_at(0, r ^ flip), plan.part)
        pairs.append((wide.at[i * plan.part : (i + 1) * plan.part], out.at[pl.ds(start, plan.part)]))
    finish(launch(pairs, sems))


def hand_on_kernel(after, block, out):
    rows = out.shape[0]
    out[...] = block[rows:]


def nothing(*refs):
    pass


def gate(array, *waits, weight=0, spec=ANY):
    operand = pltpu.with_memory_space_constraint(array, pltpu.VMEM)
    if spec is HBM:
        waits = [pltpu.with_memory_space_constraint(wait, pltpu.HBM) for wait in waits]
    return pl.pallas_call(
        nothing,
        out_shape=pltpu.VMEM(array.shape, array.dtype),
        in_specs=[VMEM] + [spec] * len(waits),
        out_specs=VMEM,
        input_output_aliases={0: 0},
        compiler_params=PARAMS,
        cost_estimate=pl.CostEstimate(flops=weight, bytes_accessed=0, transcendentals=0),
        name="gate",
    )(operand, *waits)


def call(kernel, name, ins, in_specs, shapes, out_spec, scratch=(), copies=0, loose=0, weight=0, alias=()):
    sems = [pltpu.SemaphoreType.DMA((copies,))] if copies else []
    spaces = {id(HBM): pltpu.HBM, id(VMEM): pltpu.VMEM}
    ins = [
        pltpu.with_memory_space_constraint(a, spaces[id(spec)]) if id(spec) in spaces else a
        for a, spec in zip(ins, in_specs)
    ]
    shapes = [pltpu.VMEM(a.shape, a.dtype) if i >= loose else a for i, a in enumerate(shapes)]
    return pl.pallas_call(
        kernel,
        out_shape=tuple(shapes),
        in_specs=in_specs,
        out_specs=tuple([out_spec] * len(shapes)),
        scratch_shapes=list(scratch) + sems,
        input_output_aliases=dict(alias),
        compiler_params=PARAMS,
        cost_estimate=pl.CostEstimate(flops=weight, bytes_accessed=0, transcendentals=0),
        name=name,
    )(*ins)


def body(ranks, shards, layer_input, queries, d_out, segment_ids, kv_weight):
    rows, width = layer_input.shape
    deep, cols = kv_weight.shape
    plan = Plan(ranks, shards, rows, width, deep, cols)
    group, half, part = plan.group, plan.half, plan.part
    lines = shards // 2
    r = lax.axis_index("rep")
    shape = jax.ShapeDtypeStruct

    def swap(array, axis, flip):
        size = ranks if axis == "rep" else shards
        return lax.ppermute(array, axis, [(i, i ^ flip) for i in range(size)])

    full = shape((rows, plan.near_width + plan.far_width), BF16)
    others = group - 2
    blocks = plan.blocks
    cuts = call(
        functools.partial(cut_kernel, plan), "cut", [layer_input, kv_weight], [HBM] * 2,
        [shape((half, cols), BF16), shape((part, cols), BF16)]
        + [shape((others * rows, plan.far_width), BF16)] * blocks,
        VMEM, copies=2 + others * plan.far,
    )
    own_half, own_part = cuts[:2]

    def hand_on(block, after, weight):
        half_block = shape((rows, block.shape[1]), BF16)
        mine = call(
            hand_on_kernel, "hand_on", [after, block], [ANY, VMEM], [half_block], VMEM, weight=weight
        )[0]
        return [block, swap(mine, "rep", 1)]

    def write(flips, terms, given=(), waits=()):
        return call(
            functools.partial(rows_kernel, plan, flips), "rows", [*given, *waits, *terms],
            [HBM] * len(given) + [ANY] * len(waits) + [VMEM] * len(terms),
            [shape((deep, cols), F32)], HBM,
            scratch=[pltpu.VMEM((len(flips) * part, cols), F32)], copies=len(flips), loose=1,
            alias={0: 0} if given else {},
        )[0]

    def cross(pieces, *waits):
        return [swap(gate(p, *waits) if waits else p, "rep", 2) for p in pieces]

    far_cross = cross(cuts[2:])
    beside = swap(own_half, "shard", 1)
    ahead = swap(own_part, "shard", 2)
    apart = [swap(own_part, "shard", 2 * d) for d in range(2, lines)]
    near = [own_half, beside]
    far = [a for piece in (ahead, *apart) for a in (piece, swap(piece, "shard", 1))]
    corner = far[1]
    far_x = []
    for block in far_cross:
        far_x += hand_on(block, corner, FRONT)

    stacked = shape((QH * rows, HEAD), BF16)
    staged = call(
        functools.partial(stage_kernel, plan), "stage",
        [layer_input, queries, d_out, segment_ids.reshape(rows, 1), segment_ids],
        [HBM] * 3 + [VMEM] * 2,
        [full, stacked, stacked, shape((rows, rows), F32), full]
        + [shape((rows, NEAR * part), BF16)] * others,
        VMEM, copies=2 * shards + others * NEAR + 2 * QH, weight=SLIGHT,
    )
    own, qs, dos, mask = staged[:4]
    partner = swap(gate(staged[4], apart[0], corner, beside), "rep", 1)

    low = shape((rows, cols), BF16)
    terms = list(call(
        functools.partial(project_kernel, plan), "project",
        [own, partner, *far_x[:1], *near, *far], [VMEM] * (2 + blocks + NEAR + plan.far),
        [shape((rows, cols), F32)] + [low] * (1 + blocks), VMEM, weight=FRONT,
    ))
    for handed in far_x[1:]:
        terms += call(
            functools.partial(project_last_kernel, plan), "project_last",
            [terms[0], handed, *far], [ANY] + [VMEM] * (1 + plan.far), [low], VMEM,
        )
    terms = [terms[0]] + [swap(terms[d], "rep", d) for d in range(1, group)]

    near_x = [swap(gate(a, corner), "rep", 2) for a in staged[5:6]]
    d_queries, d_keyval = call(
        functools.partial(attention_kernel, group), "attention",
        [qs, dos, mask, *terms, *near_x], [VMEM] * (3 + group) + [ANY] * blocks,
        [shape(queries.shape, BF16), shape((rows, cols), BF16)], VMEM, loose=1, weight=FRONT,
    )

    grads = [d_keyval] + [swap(d_keyval, "rep", d) for d in range(1, group)]
    block = shape((part, cols), BF16)
    mine = call(
        functools.partial(gather_kernel, plan), "gather", [grads[1], *far], [ANY] + [VMEM] * plan.far,
        [shape((plan.far * part, cols), BF16)], VMEM,
    )
    far_rows_all = [*mine, *cross(list(mine) * blocks)]
    sums = []
    for places, outs in (
        ({5: (0, 0), 4: (1, 0)}, [block] * 2),
        (
            {2: (0, 0), 3: (0, 1), **{e: (e - 5, 0) for e in range(6, shards)}},
            [shape((2 * part, cols), BF16)] + [block] * (shards - 6),
        ),
    ):
        sums += call(
            functools.partial(weight_grad_kernel, plan, places), "weight_grad",
            [own, partner, *far_x, *grads, *sums], [VMEM] * (2 * group) + [ANY] * len(sums), outs, VMEM,
            weight=0 if sums else FRONT,
        )
    sums = {e: term for e, term in zip((5, 4, 2, *range(6, shards)), sums)}
    near_x += [swap(gate(a, d_keyval), "rep", 3) for a in staged[6:]]
    held = []

    beyond = swap(gate(sums[2], *near_x[1:]), "shard", 2)

    def pair(d):
        term = sums[2 * d + 1]
        came = swap(gate(term, *near_x[1:]) if d > 2 else term, "shard", 1)
        mine = gate(sums[2 * d], *held[-1:], weight=SLIGHT // 2)
        out = call(pair_kernel, "pair", [mine, came], [VMEM] * 2, [block], VMEM)[0]
        held.append(out)
        return out

    pairs = {d: pair(d) for d in range(2, lines)}
    total = [swap(pairs[d], "shard", 2 * d) for d in range(2, lines)]
    near_terms = call(
        functools.partial(weight_grad_kernel, plan, {0: (0, 0), 1: (1, 0)}), "weight_grad_near",
        [own, partner, *near_x, *grads, pairs[2]], [VMEM] * (2 * group) + [ANY], [block] * 2, VMEM,
    )
    keep, send = call(
        near_kernel, "near", [*near_terms, beyond], [VMEM] * 3, [shape((part, cols), F32), block], VMEM
    )
    total.append(swap(gate(send, pairs[lines - 1]), "shard", 1))
    again = ranks > group
    quarter = call(
        total_kernel, "total", [keep, *total], [VMEM] * (1 + len(total)),
        [shape((part, cols), F32 if again else BF16)], VMEM,
    )[0]
    if again:
        rings = [[g + group * k for k in range(ranks // group)] for g in range(group)]
        quarter = lax.psum(quarter, "rep", axis_index_groups=rings).astype(BF16)
    halves = shape((rows, shards * half), BF16)
    backs = call(
        functools.partial(input_grad_kernel, plan), "input_grad",
        [quarter, *grads[:2], *near, *far_rows_all], [ANY] + [VMEM] * (3 + NEAR + blocks),
        [halves] * 2, VMEM,
    )
    backs = [backs[0], swap(backs[1], "rep", 1)]
    quarters = [quarter, swap(quarter, "rep", 1)]
    d_kv_weight = write(range(2), quarters, waits=backs[:1])
    for crossing in cross([quarter] * blocks):
        crossing = gate(crossing, d_kv_weight, weight=FRONT, spec=HBM)
        quarters += [crossing, swap(crossing, "rep", 1)]
    d_input = call(
        functools.partial(place_kernel, plan), "place", backs, [VMEM] * 2,
        [shape((rows, width), BF16)], HBM, copies=2 * shards, loose=1, weight=FRONT,
    )[0]
    if group > 2:
        d_kv_weight = write(range(2, group), quarters[2:], [d_kv_weight, d_input])
    return (d_input, d_queries, d_kv_weight)


def solution(mesh):
    ranks, shards = mesh.shape["rep"], mesh.shape["shard"]
    spread = P(("rep", "shard"), None)
    return jax.shard_map(
        functools.partial(body, ranks, shards),
        mesh=mesh,
        in_specs=(spread, spread, spread, spread, P("shard", None)),
        out_specs=(spread, spread, P("shard", None)),
        check_vma=False,
    )
```
